256 devices in a mesh: blk: 32 (over z, y_hi, core), group: 8 (over x, y_lo).
Axes of the slice: x: 4, y: 4 (y_hi: 2, y_lo: 2; y = y_hi * 2 + y_lo), z: 8, core: 2. Of those that a mesh axis runs over, the one named last changes fastest.
Arguments:
- image_embed: bfloat16 [163840, 1152], P(('blk', 'group')), may hold values from -0.1796875 to 0.1796875
- text_embed: bfloat16 [163840, 1152], P(('blk', 'group')), may hold values from -0.1796875 to 0.1796875
- text_bits: int32 [163840, 1152], P(('blk', 'group')), may hold values from 0 to 4095
- labels: int32 [163840], replicated, may hold values from 0 to 2559
- scale: float32 [], replicated, may hold values from 4 to 12
- bias: float32 [], replicated, may hold values from -3 to -1
Outputs:
- grad_image: bfloat16 [163840, 1152], P(('blk', 'group'))
- grad_text: bfloat16 [163840, 1152], P(('blk', 'group'))
The draws below stay inside these ranges and needn't reach their ends.
All inputs are finite; a program needn't handle non-finite values.
Results may differ from the reference program's by a relative error of at most 0.0065.
Values may be sent and summed in bfloat16 or wider, within the bound.
A program may use at most 128 MiB of HBM per device.

```python
import jax
import jax.numpy as jnp
from jax import lax

D = 1152
ROWS = 640
BATCH = 163840
N_BLK = 32
N_GROUP = 8


def plant(drawn, own_key, smallest, largest):
    longest = drawn.shape.index(max(drawn.shape))
    spots = []
    for shift in (0, 1):
        where = [jax.random.randint(jax.random.fold_in(own_key, axis), (), 0, length) for axis, length in enumerate(drawn.shape)]
        where[longest] = (where[longest] + shift) % drawn.shape[longest]
        spots.append(tuple(where))
    return drawn.at[spots[0]].set(smallest).at[spots[1]].set(largest)


def levels(stream_key, extent, cuts, smallest, high):
    loudness, own = 1.0, jax.random.fold_in(stream_key, 6)
    for position, shards_of in cuts:
        draws = jnp.exp(jax.random.uniform(jax.random.fold_in(own, position), (shards_of,), jnp.float32, smallest / len(cuts), high / len(cuts)))
        loudness = loudness * jnp.repeat(draws, extent[position] // shards_of).reshape([-1 if axis == position else 1 for axis in range(len(extent))])
    return loudness


def centred(key, shape, spread, limit, pieces=(), held_as=jnp.bfloat16):
    loudness = levels(key, shape, pieces, -0.22, 0.18) if pieces else 1.0
    entries = jax.random.normal(key, shape, jnp.float32) * spread * loudness
    return jnp.minimum(jnp.maximum(entries, -limit), limit).astype(held_as)


def setup_inputs(seed: int = 0) -> dict:
    seeds = jax.random.split(jax.random.key(seed), 7)
    return {
        "image_embed": centred(seeds[0], (BATCH, D), 0.03, 0.1796875, ((0, 256),)),
        "text_embed": centred(seeds[1], (BATCH, D), 0.03, 0.1796875, ((0, 256),)),
        "text_bits": plant(jax.random.randint(seeds[2], (BATCH, D), 0, 4096), jax.random.fold_in(seeds[2], 1), 0, 4095).astype(jnp.int32),
        "labels": plant(jax.random.randint(seeds[3], (BATCH,), 0, 4 * ROWS), jax.random.fold_in(seeds[3], 1), 0, (4 * ROWS) - 1).astype(jnp.int32),
        "scale": jnp.clip(jax.random.uniform(seeds[4], (), jnp.float32, 4.0, 12.0), 4.0, 12.0),
        "bias": jnp.clip(jax.random.uniform(seeds[5], (), jnp.float32, -3.0, -1.0), -3.0, -1.0),
    }


EPS = 1e-06

def unit_rows(values):
    full = values.astype(jnp.float32)
    inverse = lax.rsqrt(lax.optimization_barrier(jnp.sum(full * full, axis=-1, keepdims=True)) + EPS)
    return (full * inverse, inverse)

def quantize(text_embed, text_bits):
    noise = (text_bits.astype(jnp.float32) + 0.5) / 4096.0
    return jnp.floor(text_embed.astype(jnp.float32) * 128.0 + noise) / 128.0

def pair_dot(left, right):
    return lax.dot_general(left, right, (((1,), (1,)), ((), ())), preferred_element_type=jnp.float32)

def coefficient(left_half, right_half, left_labels, right_labels, scale, bias):
    logit = scale * pair_dot(left_half, right_half) + bias
    sign = jnp.where(left_labels[:, None] == right_labels[None, :], 1.0, -1.0).astype(jnp.float32)
    return (-sign * scale * jax.nn.sigmoid(-sign * logit)).astype(jnp.bfloat16)

def reference(image_embed, text_embed, text_bits, labels, scale, bias):
    blocks = N_BLK * N_GROUP
    image_unit, image_inv = unit_rows(image_embed)
    text_unit, text_inv = unit_rows(quantize(text_embed, text_bits))
    image_half = image_unit.astype(jnp.bfloat16).reshape(blocks, ROWS, D)
    text_half = text_unit.astype(jnp.bfloat16).reshape(blocks, ROWS, D)
    block_labels = labels.reshape(blocks, ROWS)

    def block_of(cycle_pos, group_pos):
        return ((cycle_pos + N_BLK) % N_BLK * N_GROUP + (group_pos + N_GROUP) % N_GROUP).astype(jnp.int32)

    def one_block(number):
        cycle_pos = number // N_GROUP
        group_pos = number % N_GROUP
        own_image = image_half[number]
        own_text = text_half[number]
        own_labels = block_labels[number]
        own_coef = coefficient(own_image, own_text, own_labels, own_labels, scale, bias)
        image_sum = jnp.dot(own_coef, own_text, preferred_element_type=jnp.float32)
        text_sum = lax.dot_general(own_coef, own_image, (((0,), (0,)), ((), ())), preferred_element_type=jnp.float32)
        text_sources = [block_of(cycle_pos - 1, group_pos), block_of(cycle_pos + 1, group_pos), block_of(cycle_pos, group_pos - 1)]
        image_sources = [block_of(cycle_pos - 1, group_pos), block_of(cycle_pos + 1, group_pos), block_of(cycle_pos, group_pos + 1)]
        for source in text_sources:
            other_text = text_half[source]
            other_coef = coefficient(own_image, other_text, own_labels, block_labels[source], scale, bias)
            image_sum = image_sum + jnp.dot(other_coef, other_text, preferred_element_type=jnp.float32)
        for source in image_sources:
            other_image = image_half[source]
            other_coef = coefficient(own_text, other_image, own_labels, block_labels[source], scale, bias)
            partial_term = jnp.dot(other_coef, other_image, preferred_element_type=jnp.float32).astype(jnp.bfloat16)
            text_sum = text_sum + partial_term.astype(jnp.float32)
        return (image_sum, text_sum)
    image_sums, text_sums = lax.map(one_block, jnp.arange(blocks, dtype=jnp.int32))
    image_sums = image_sums.reshape(BATCH, D)
    text_sums = text_sums.reshape(BATCH, D)
    grad_image = (image_sums - image_unit * lax.optimization_barrier(jnp.sum(image_unit * image_sums, axis=-1, keepdims=True))) * image_inv
    grad_text = (text_sums - text_unit * lax.optimization_barrier(jnp.sum(text_unit * text_sums, axis=-1, keepdims=True))) * text_inv
    return (grad_image.astype(jnp.bfloat16), grad_text.astype(jnp.bfloat16))
```

```python
import functools

import jax
import jax.numpy as jnp
from jax import lax
from jax.experimental import pallas as pl
from jax.experimental.pallas import tpu as pltpu
from jax.sharding import PartitionSpec as P

EPS = 1e-06
LOG2E = 1.4426950408889634
MESH = pl.DeviceIdType.MESH

ROWS = 640
D = 1152
CHUNK = 128
SUB = 32
UNIT = ROWS // SUB
TILE = 320
PREP = 64
SET = 4 * ROWS
SPARE = 2 * SET
LAB = ROWS // 128


def kernel(
    n_blk,
    n_group,
    image_ref,
    text_ref,
    bits_ref,
    labels_ref,
    scale_ref,
    bias_ref,
    grad_image_ref,
    grad_text_ref,
    held,
    raw_image,
    raw_text,
    bits,
    labels,
    column,
    inverse,
    total,
    result,
    load_sem,
    label_sem,
    store_sem,
    near_send,
    near_recv,
    first_send,
    first_recv,
    far_send,
    far_recv,
    side_send,
    side_recv,
):
    b = lax.axis_index("blk")
    g = lax.axis_index("group")
    core = b % 2
    low = g % 2
    twin = b + 1 - 2 * core
    beyond = (b + 2 * core - 1 + n_blk) % n_blk
    mate = g + 1 - 2 * low
    side_to = (g + 2 - 4 * low + n_group) % n_group
    side_from = (g - 2 + 4 * low + n_group) % n_group
    near_dev, first_dev = (twin, g), (b, mate)
    far_dev, side_dev, source_dev = (beyond, mate), (b, side_to), (b, side_from)

    def load(array, to, piece, sems):
        rows = pl.ds(piece * PREP, PREP)
        return pltpu.make_async_copy(array.at[rows], to.at[rows], sems.at[piece])

    pieces = ROWS // PREP
    loads = ((image_ref, raw_image), (text_ref, raw_text), (bits_ref, bits))
    for which, (array, to) in enumerate(loads):
        for piece in range(pieces):
            load(array, to, piece, load_sem.at[which]).start()
    label_copy = pltpu.make_async_copy(labels_ref, labels, label_sem)
    label_copy.start()

    barrier = pltpu.get_barrier_semaphore()
    for device in (near_dev, first_dev, far_dev, source_dev):
        pl.semaphore_signal(barrier, inc=1, device_id=device, device_id_type=MESH)

    def remote(src, dst, send, recv, device):
        return pltpu.make_async_remote_copy(
            src_ref=held.at[src],
            dst_ref=held.at[dst],
            send_sem=send,
            recv_sem=recv,
            device_id=device,
            device_id_type=MESH,
        )

    def span(start, size):
        return pl.ds(pl.multiple_of(start, 16), size)

    def first_row(h, to_low):
        texts = h // UNIT
        at = h - texts * UNIT
        chunk = at // (CHUNK // SUB)
        inside = (at - chunk * (CHUNK // SUB)) * SUB
        used = texts * to_low + (1 - texts) * (1 - to_low)
        there = (1 - texts) * SET + 2 * ROWS + chunk * 2 * CHUNK + CHUNK
        return used * there + (1 - used) * (SPARE + chunk * CHUNK) + inside

    def first(h):
        texts = h // UNIT
        at = h - texts * UNIT
        return remote(
            span((1 - texts) * SET + at * SUB, SUB),
            span(first_row(h, 1 - low), SUB),
            first_send,
            first_recv.at[h],
            first_dev,
        )

    def landing(h):
        texts = h // UNIT
        at = h - texts * UNIT
        chunk = at // (CHUNK // SUB)
        inside = (at - chunk * (CHUNK // SUB)) * SUB
        return texts, chunk, (1 - texts) * SET + 2 * ROWS + chunk * 2 * CHUNK + inside

    def far(h):
        texts, chunk, row = landing(h)
        return remote(
            span(first_row(h, low), SUB),
            span(row, SUB),
            far_send,
            far_recv.at[texts * LAB + chunk],
            far_dev,
        )

    def side(h):
        texts, chunk, row = landing(h)
        return remote(
            span(first_row(h, low), SUB),
            span(row + CHUNK, SUB),
            side_send,
            side_recv.at[chunk],
            side_dev,
        )

    def near(texts):
        start = (1 - texts) * SET
        return remote(
            span(start, ROWS),
            span(start + ROWS, ROWS),
            near_send.at[texts],
            near_recv.at[texts],
            near_dev,
        )

    def unit_rows(full, row, which, base):
        inv = lax.rsqrt(jnp.sum(full * full, axis=-1, keepdims=True) + EPS)
        inverse[which, pl.ds(row, PREP), :] = inv
        held[pl.ds(base + row, PREP), :] = (full * inv).astype(jnp.bfloat16)

    def prepare_image(piece):
        load(image_ref, raw_image, piece, load_sem.at[0]).wait()
        row = pl.multiple_of(piece * PREP, PREP)
        unit_rows(raw_image[pl.ds(row, PREP), :].astype(jnp.float32), row, 0, SET)

    def prepare_text(piece):
        load(text_ref, raw_text, piece, load_sem.at[1]).wait()
        load(bits_ref, bits, piece, load_sem.at[2]).wait()
        row = pl.multiple_of(piece * PREP, PREP)
        rows = pl.ds(row, PREP)
        noise = (bits[rows, :].astype(jnp.float32) + 0.5) * (1.0 / 4096.0)
        full = jnp.floor(raw_text[rows, :].astype(jnp.float32) * 128.0 + noise) * (1.0 / 128.0)
        raw_text[rows, :] = full.astype(jnp.bfloat16)
        unit_rows(full, row, 1, 0)

    def clear(i, _):
        total[0, pl.ds(pl.multiple_of(i * PREP, PREP), PREP), :] = jnp.zeros((PREP, D), jnp.float32)
        total[1, pl.ds(pl.multiple_of(i * PREP, PREP), PREP), :] = jnp.zeros((PREP, D), jnp.float32)
        return 0

    prepare_image(0)
    pl.semaphore_wait(barrier, 4)

    per = PREP // SUB

    def image_step(piece, _):
        def send(i, _):
            first(piece * per + i).start()
            return 0

        lax.fori_loop(0, per, send, 0)

        @pl.when(piece + 1 < pieces)
        def _():
            prepare_image(piece + 1)

        return 0

    lax.fori_loop(0, pieces, image_step, 0)
    near(0).start()

    def text_step(piece, _):
        prepare_text(piece)

        def send(i, _):
            first(UNIT + piece * per + i).start()
            return 0

        lax.fori_loop(0, per, send, 0)
        return 0

    lax.fori_loop(0, pieces, text_step, 0)
    near(1).start()

    label_copy.wait()
    number = b * n_group + g
    for part in range(LAB):
        row = jnp.broadcast_to(labels[pl.ds(number * LAB + part, 1), :], (128, 128))
        column[pl.ds(part * 128, 128), :] = row.T

    lax.fori_loop(0, pieces, clear, 0)

    scale = scale_ref[0]
    slope = scale * LOG2E
    shift = bias_ref[0] * LOG2E
    below = (g - 1 + n_group) % n_group
    above = (g + 1) % n_group

    def pump(h):
        first(h).wait_recv()
        far(h).start()

        @pl.when(h // UNIT == 1 - low)
        def _():
            side(h).start()

    def meet(which, j, tile):
        far_chunk = j // LAB
        k = j - far_chunk * LAB
        own_part = 2 * k
        group = which * above + (1 - which) * below
        a_near = own_part // LAB
        b_near = (own_part + 1) // LAB
        num_a = (b + (twin - b) * a_near) * n_group + g
        num_b = (b + (twin - b) * b_near) * n_group + g
        row_a = num_a * LAB + own_part - a_near * LAB
        row_b = num_b * LAB + own_part + 1 - b_near * LAB
        far_a = (beyond * n_group + g) * LAB + k
        far_b = (b * n_group + group) * LAB + k
        row_a = row_a + (far_a - row_a) * far_chunk
        row_b = row_b + (far_b - row_b) * far_chunk
        them_rows = span(which * SET + j * 2 * CHUNK, 2 * CHUNK)
        own_rows = span((1 - which) * SET + tile * TILE, TILE)
        acc_rows = span(tile * TILE, TILE)
        dots = lax.dot_general(
            held[own_rows, :],
            held[them_rows, :],
            (((1,), (1,)), ((), ())),
            preferred_element_type=jnp.float32,
        )
        power = dots * slope + shift
        mine = column[acc_rows, :]
        same_a = mine == labels[pl.ds(row_a, 1), :]
        same_b = mine == labels[pl.ds(row_b, 1), :]
        same = jnp.concatenate([same_a, same_b], axis=1)
        coef = jnp.where(same, -scale, scale) / (1.0 + jnp.exp2(jnp.where(same, power, -power)))
        total[which, acc_rows, :] += lax.dot_general(
            coef.astype(jnp.bfloat16),
            held[them_rows, :],
            (((1,), (0,)), ((), ())),
            preferred_element_type=jnp.float32,
        )

    def finish(which, piece):
        row = pl.multiple_of(piece * PREP, PREP)
        rows = pl.ds(row, PREP)
        inv = inverse[which, rows, :]
        raw = raw_image if which == 0 else raw_text
        out = grad_image_ref if which == 0 else grad_text_ref
        unit = raw[rows, :].astype(jnp.float32) * inv
        sums = total[which, rows, :]
        along = jnp.sum(unit * sums, axis=-1, keepdims=True)
        result[which, rows, :] = ((sums - unit * along) * inv).astype(jnp.bfloat16)
        store(which, piece).start()

    def store(which, piece):
        out = grad_image_ref if which == 0 else grad_text_ref
        rows = pl.ds(piece * PREP, PREP)
        return pltpu.make_async_copy(result.at[which, rows], out.at[rows], store_sem.at[which, piece])

    def whole(start, size, send, recv):
        return remote(span(start, size), span(start, size), send, recv, first_dev)

    def landed(texts, k):
        base = (1 - texts) * SET + 2 * ROWS + k * 2 * CHUNK
        whole(base, CHUNK, far_send, far_recv.at[texts * LAB + k]).wait_recv()

        @pl.when(low == 1 - texts)
        def _():
            whole(base + CHUNK, CHUNK, side_send, side_recv.at[k]).wait_recv()

    tiles = ROWS // TILE

    def early(h, _):
        pump(h)
        p = h // tiles
        tile = h - p * tiles

        @pl.when(h == 4 * tiles)
        def _():
            near(0).wait_recv()
            near(1).wait_recv()

        meet(1 - p % 2, p // 2, tile)
        return 0

    lax.fori_loop(0, 2 * LAB * tiles, early, 0)
    done = 2 * LAB * tiles

    def middle(i, _):
        pump(done + i)
        k = i // tiles
        tile = i - k * tiles

        @pl.when(tile == 0)
        def _():
            landed(0, k)

        meet(1, LAB + k, tile)
        return 0

    lax.fori_loop(0, LAB * tiles, middle, 0)
    done = done + LAB * tiles

    def late(i, _):
        k = i // tiles
        tile = i - k * tiles

        @pl.when(i < 6)
        def _():
            pump(done + i)

        @pl.when((i >= 6) & (i < 8))
        def _():
            pump(done + 6 + 2 * (i - 6))
            pump(done + 7 + 2 * (i - 6))

        finish(1, i)

        @pl.when(tile == 0)
        def _():
            landed(1, k)

        meet(0, LAB + k, tile)
        return 0

    lax.fori_loop(0, LAB * tiles, late, 0)

    def last(piece, _):
        finish(0, piece)
        return 0

    lax.fori_loop(0, pieces, last, 0)

    near(0).wait_send()
    near(1).wait_send()
    whole(0, 2 * ROWS, first_send, first_recv.at[0]).wait_send()
    whole(0, 2 * ROWS, far_send, first_recv.at[0]).wait_send()
    whole(0, ROWS, side_send, first_recv.at[0]).wait_send()

    def stored(piece, _):
        store(0, piece).wait()
        store(1, piece).wait()
        return 0

    lax.fori_loop(0, pieces, stored, 0)


def shards(n_blk, n_group, image_embed, text_embed, text_bits, labels, scale, bias):
    dma = pltpu.SemaphoreType.DMA
    pieces = ROWS // PREP
    return pl.pallas_call(
        functools.partial(kernel, n_blk, n_group),
        out_shape=(
            jax.ShapeDtypeStruct((ROWS, D), jnp.bfloat16),
            jax.ShapeDtypeStruct((ROWS, D), jnp.bfloat16),
        ),
        in_specs=[pl.BlockSpec(memory_space=pl.ANY)] * 4
        + [pl.BlockSpec(memory_space=pltpu.SMEM)] * 2,
        out_specs=(pl.BlockSpec(memory_space=pl.ANY), pl.BlockSpec(memory_space=pl.ANY)),
        scratch_shapes=[
            pltpu.VMEM((SPARE + ROWS, D), jnp.bfloat16),
            pltpu.VMEM((ROWS, D), jnp.bfloat16),
            pltpu.VMEM((ROWS, D), jnp.bfloat16),
            pltpu.VMEM((ROWS, D), jnp.int32),
            pltpu.VMEM((labels.shape[0] // 128, 128), jnp.int32),
            pltpu.VMEM((ROWS, 128), jnp.int32),
            pltpu.VMEM((2, ROWS, 1), jnp.float32),
            pltpu.VMEM((2, ROWS, D), jnp.float32),
            pltpu.VMEM((2, ROWS, D), jnp.bfloat16),
            dma((3, pieces)),
            dma,
            dma((2, pieces)),
            dma((2,)),
            dma((2,)),
            dma,
            dma((2 * UNIT,)),
            dma,
            dma((2 * LAB,)),
            dma,
            dma((LAB,)),
        ],
        compiler_params=pltpu.CompilerParams(
            collective_id=0, has_side_effects=True, vmem_limit_bytes=48 * 1024 * 1024
        ),
    )(
        image_embed,
        text_embed,
        text_bits,
        labels.reshape(-1, 128),
        scale.reshape(1),
        bias.reshape(1),
    )


def solution(mesh):
    rows = P(("blk", "group"), None)
    return jax.shard_map(
        functools.partial(shards, mesh.shape["blk"], mesh.shape["group"]),
        mesh=mesh,
        in_specs=(rows, rows, rows, P(), P(), P()),
        out_specs=(rows, rows),
        check_vma=False,
    )
```

```python
import functools

import jax
import jax.numpy as jnp
from jax import lax
from jax.experimental import pallas as pl
from jax.experimental.pallas import tpu as pltpu
from jax.sharding import PartitionSpec as P

EPS = 1e-06
LOG2E = 1.4426950408889634
MESH = pl.DeviceIdType.MESH

ROWS = 640
D = 1152
HALF = 64
PAIR = 2 * HALF
SUB = 32
UNIT = ROWS // SUB
WIDE = 256
PREP = 128
STEP = 32
SET = 4 * ROWS
SPARE = 2 * SET
LAB = ROWS // 128
HALVES = ROWS // HALF
PAIRS = SET // PAIR
CHUNK = 2 * PAIR


def kernel(
    n_blk,
    n_group,
    image_ref,
    text_ref,
    bits_ref,
    labels_ref,
    scale_ref,
    bias_ref,
    grad_text,
    sums_image,
    raw_image,
    inverse_image,
    held,
    raw_text,
    bits,
    labels,
    column,
    table,
    inverse_text,
    sums_text,
    coefs,
    load_sem,
    label_sem,
    near_send,
    near_recv,
    first_send,
    first_recv,
    far_send,
    far_recv,
    side_send,
    side_recv,
):
    b = lax.axis_index("blk")
    g = lax.axis_index("group")
    core = b % 2
    low = g % 2
    twin = b + 1 - 2 * core
    beyond = (b + 2 * core - 1 + n_blk) % n_blk
    mate = g + 1 - 2 * low
    side_to = (g + 2 - 4 * low + n_group) % n_group
    side_from = (g - 2 + 4 * low + n_group) % n_group
    near_dev, first_dev = (twin, g), (b, mate)
    far_dev, side_dev, source_dev = (beyond, mate), (b, side_to), (b, side_from)

    barrier = pltpu.get_barrier_semaphore()
    for device in (near_dev, first_dev, far_dev, source_dev):
        pl.semaphore_signal(barrier, inc=1, device_id=device, device_id_type=MESH)

    def load(array, to, piece, sems):
        rows = pl.ds(piece * PREP, PREP)
        return pltpu.make_async_copy(array.at[rows], to.at[rows], sems.at[piece])

    pieces = ROWS // PREP
    loads = ((image_ref, raw_image), (text_ref, raw_text), (bits_ref, bits))
    for which, (array, to) in enumerate(loads):
        for piece in range(pieces):
            load(array, to, piece, load_sem.at[which]).start()
    label_copy = pltpu.make_async_copy(labels_ref, labels, label_sem)
    label_copy.start()

    def remote(src, dst, send, recv, device):
        return pltpu.make_async_remote_copy(
            src_ref=held.at[src],
            dst_ref=held.at[dst],
            send_sem=send,
            recv_sem=recv,
            device_id=device,
            device_id_type=MESH,
        )

    def span(start, size):
        return pl.ds(pl.multiple_of(start, 16), size)

    def landing(h):
        texts = h // UNIT
        at = h - texts * UNIT
        half = at // (HALF // SUB)
        inside = (at - half * (HALF // SUB)) * SUB
        return texts, half, (1 - texts) * SET + 2 * ROWS + half * PAIR + inside

    def first_row(h, to_low):
        texts, _, row = landing(h)
        at = h - texts * UNIT
        used = texts * to_low + (1 - texts) * (1 - to_low)
        return used * (row + HALF) + (1 - used) * (SPARE + at * SUB)

    def first(h):
        texts = h // UNIT
        at = h - texts * UNIT
        return remote(
            span((1 - texts) * SET + at * SUB, SUB),
            span(first_row(h, 1 - low), SUB),
            first_send,
            first_recv.at[h],
            first_dev,
        )

    def far(h):
        texts, half, row = landing(h)
        return remote(
            span(first_row(h, low), SUB),
            span(row, SUB),
            far_send,
            far_recv.at[texts * HALVES + half],
            far_dev,
        )

    def side(h):
        texts, half, row = landing(h)
        return remote(
            span(first_row(h, low), SUB),
            span(row + HALF, SUB),
            side_send,
            side_recv.at[half],
            side_dev,
        )

    def near(texts):
        start = (1 - texts) * SET
        return remote(
            span(start, ROWS),
            span(start + ROWS, ROWS),
            near_send.at[texts],
            near_recv.at[texts],
            near_dev,
        )

    def unit_rows(fulls, steps, inverse, base):
        invs = [
            lax.rsqrt(jnp.sum(jnp.square(full()), axis=-1, keepdims=True) + EPS) for full in fulls
        ]
        for full, inv, row in zip(fulls, invs, steps):
            inverse[pl.ds(row, STEP), :] = inv
            held[pl.ds(base + row, STEP), :] = (full() * inv).astype(jnp.bfloat16)

    def steps_of(row, size):
        return [pl.multiple_of(row + at, STEP) for at in range(0, size, STEP)]

    def loader(array, row):
        return lambda: array[pl.ds(row, STEP), :].astype(jnp.float32)

    def image_rows(row, size):
        steps = steps_of(row, size)
        unit_rows([loader(raw_image, at) for at in steps], steps, inverse_image, SET)

    def text_rows(row, size):
        steps = steps_of(row, size)
        for at in steps:
            rows = pl.ds(at, STEP)
            noise = (bits[rows, :].astype(jnp.float32) + 0.5) * (1.0 / 4096.0)
            full = jnp.floor(raw_text[rows, :].astype(jnp.float32) * 128.0 + noise) * (1.0 / 128.0)
            raw_text[rows, :] = full.astype(jnp.bfloat16)
        unit_rows([loader(raw_text, at) for at in steps], steps, inverse_text, 0)

    per = PREP // SUB

    def send(h, _):
        first(h).start()
        return 0

    load(image_ref, raw_image, 0, load_sem.at[0]).wait()
    image_rows(0, STEP)
    pl.semaphore_wait(barrier, 4)
    lax.fori_loop(0, STEP // SUB, send, 0)
    for row in range(STEP, PREP, STEP):
        image_rows(row, STEP)
        lax.fori_loop(row // SUB, (row + STEP) // SUB, send, 0)

    def image_step(piece, _):
        load(image_ref, raw_image, piece, load_sem.at[0]).wait()
        image_rows(piece * PREP, PREP)
        lax.fori_loop(piece * per, (piece + 1) * per, send, 0)
        return 0

    lax.fori_loop(1, pieces, image_step, 0)
    near(0).start()

    def pump(h):
        first(h).wait_recv()
        far(h).start()

        @pl.when(h // UNIT == 1 - low)
        def _():
            side(h).start()

    def pumps(start, stop):
        def one(h, _):
            pump(h)
            return 0

        lax.fori_loop(start, stop, one, 0)

    pumps(0, 1)

    def text_step(piece, _):
        load(text_ref, raw_text, piece, load_sem.at[1]).wait()
        load(bits_ref, bits, piece, load_sem.at[2]).wait()
        text_rows(piece * PREP, PREP)
        lax.fori_loop(UNIT + piece * per, UNIT + (piece + 1) * per, send, 0)

        @pl.when(piece % 2 == 0)
        def _():
            pump(1 + piece // 2)

        return 0

    lax.fori_loop(0, pieces, text_step, 0)
    near(1).start()

    label_copy.wait()
    number = b * n_group + g
    for part in range(LAB):
        row = jnp.broadcast_to(labels[pl.ds(number * LAB + part, 1), :], (128, 128))
        column[pl.ds(part * 128, 128), :] = row.T

    below = (g - 1 + n_group) % n_group
    above = (g + 1) % n_group
    first_half = lax.broadcasted_iota(jnp.int32, (1, PAIR), 1) < HALF

    def label_row(at_blk, at_group, part):
        return labels[pl.ds((at_blk * n_group + at_group) * LAB + part, 1), :]

    for which, other in ((0, below), (1, above)):
        for part in range(LAB):
            table[which, pl.ds(part, 1), :] = label_row(b, g, part)
            table[which, pl.ds(LAB + part, 1), :] = label_row(twin, g, part)
            far_labels = label_row(beyond, g, part)
            group_labels = label_row(b, other, part)
            table[which, pl.ds(2 * LAB + 2 * part, 1), :] = jnp.where(
                first_half, far_labels, pltpu.roll(group_labels, HALF, 1)
            )
            table[which, pl.ds(2 * LAB + 2 * part + 1, 1), :] = jnp.where(
                first_half, pltpu.roll(far_labels, HALF, 1), group_labels
            )

    scale = scale_ref[0]
    slope = scale * LOG2E
    shift = bias_ref[0] * LOG2E

    def meet(which, at, size):
        them_rows = span(which * SET + at * PAIR, size)
        own_rows = span((1 - which) * SET, ROWS)
        dots = lax.dot_general(
            held[own_rows, :],
            held[them_rows, :],
            (((1,), (1,)), ((), ())),
            preferred_element_type=jnp.float32,
        )
        power = dots * slope + shift
        mine = column[...]
        same = [mine == table[which, pl.ds(at + i, 1), :] for i in range(size // PAIR)]
        same = same[0] if size == PAIR else jnp.concatenate(same, axis=1)
        coef = jnp.where(same, -scale, scale) / (1.0 + jnp.exp2(jnp.where(same, power, -power)))
        columns = pl.ds(pl.multiple_of(at * PAIR, PAIR), size)
        coefs[which, :, columns] = coef.astype(jnp.bfloat16)

    def add_up(which, start, stop, column_at, width, fresh):
        rows = (stop - start) * PAIR
        columns = pl.ds(pl.multiple_of(column_at, 128), width)
        sums = lax.dot_general(
            coefs[which, :, pl.ds(start * PAIR, rows)],
            held[pl.ds(which * SET + start * PAIR, rows), columns],
            (((1,), (0,)), ((), ())),
            preferred_element_type=jnp.float32,
        )
        total = (sums_image, sums_text)[which]
        if not fresh:
            sums = sums + total[:, columns]
        total[:, columns] = sums

    full_columns = D // WIDE
    rest = D - full_columns * WIDE

    def whole(start, size, send, recv):
        return remote(span(start, size), span(start, size), send, recv, first_dev)

    def landed(texts, k):
        base = (1 - texts) * SET + 2 * ROWS + k * PAIR
        whole(base, HALF, far_send, far_recv.at[texts * HALVES + k]).wait_recv()

        @pl.when(low == 1 - texts)
        def _():
            whole(base + HALF, HALF, side_send, side_recv.at[k]).wait_recv()

    def meet_far(texts, k):
        landed(texts, 2 * k)
        landed(texts, 2 * k + 1)
        meet(1 - texts, 2 * LAB + 2 * k, CHUNK)

    def early(p, _):
        pump(4 + p)

        @pl.when(p == 4)
        def _():
            near(0).wait_recv()
            near(1).wait_recv()

        meet(1 - p % 2, 2 * (p // 2), CHUNK)
        return 0

    lax.fori_loop(0, 2 * LAB, early, 0)

    def far_images(k, _):
        pump(14 + k)
        meet_far(0, k)
        return 0

    lax.fori_loop(0, 3, far_images, 0)
    pumps(17, 19)

    def far_images_end(k, _):
        pumps(19 + 2 * (k - 3), 21 + 2 * (k - 3))
        meet_far(0, k)
        return 0

    lax.fori_loop(3, LAB, far_images_end, 0)

    def text_sums(n, _):
        pump(23 + n)
        add_up(1, 0, PAIRS, n * WIDE, WIDE, True)
        return 0

    lax.fori_loop(0, full_columns, text_sums, 0)
    pumps(27, 28)
    add_up(1, 0, PAIRS, full_columns * WIDE, rest, True)

    def text_out(piece, _):
        @pl.when(piece % 2 == 0)
        def _():
            pump(28 + piece // 2)

        finish_rows(raw_text, inverse_text, sums_text, grad_text, piece * PREP)
        return 0

    lax.fori_loop(0, pieces, text_out, 0)

    def far_texts(k, _):
        pump(31 + k)
        meet_far(1, k)
        return 0

    lax.fori_loop(0, 3, far_texts, 0)

    def image_sums(n, _):
        pump(34 + n)
        add_up(0, 0, PAIRS - 4, n * WIDE, WIDE, True)
        return 0

    lax.fori_loop(0, full_columns, image_sums, 0)
    pumps(38, 40)
    add_up(0, 0, PAIRS - 4, full_columns * WIDE, rest, True)

    meet_far(1, LAB - 2)
    landed(1, HALVES - 2)
    meet(0, PAIRS - 2, PAIR)
    add_up(0, PAIRS - 4, PAIRS - 1, 0, D, False)
    landed(1, HALVES - 1)
    meet(0, PAIRS - 1, PAIR)
    add_up(0, PAIRS - 1, PAIRS, 0, D, False)

    near(0).wait_send()
    near(1).wait_send()
    whole(0, 2 * ROWS, first_send, first_recv.at[0]).wait_send()
    whole(0, 2 * ROWS, far_send, first_recv.at[0]).wait_send()
    whole(0, ROWS, side_send, first_recv.at[0]).wait_send()


def finish_rows(raw, inverse, sums, out, row):
    steps = [pl.ds(pl.multiple_of(row + at, STEP), STEP) for at in range(0, PREP, STEP)]
    along = []
    for rows in steps:
        inv = inverse[rows, :]
        dot = jnp.sum(raw[rows, :].astype(jnp.float32) * sums[rows, :], axis=-1, keepdims=True)
        along.append((inv, inv * inv * dot))
    for rows, (inv, share) in zip(steps, along):
        full = raw[rows, :].astype(jnp.float32)
        out[rows, :] = ((sums[rows, :] - full * share) * inv).astype(jnp.bfloat16)


def finish_kernel(text, sums, raw, inverse, image_out, text_out, image, store_sem, text_sem):
    whole = pltpu.make_async_copy(text, text_out, text_sem)
    whole.start()

    def store(piece):
        rows = pl.ds(piece * PREP, PREP)
        return pltpu.make_async_copy(image.at[rows], image_out.at[rows], store_sem.at[piece])

    pieces = ROWS // PREP
    for piece in range(pieces):
        finish_rows(raw, inverse, sums, image, piece * PREP)
        store(piece).start()
    whole.wait()
    for piece in range(pieces):
        store(piece).wait()


def shards(n_blk, n_group, image_embed, text_embed, text_bits, labels, scale, bias):
    dma = pltpu.SemaphoreType.DMA
    pieces = ROWS // PREP
    fast = pl.BlockSpec(memory_space=pltpu.VMEM)
    parts = pl.pallas_call(
        functools.partial(kernel, n_blk, n_group),
        out_shape=(
            pltpu.VMEM((ROWS, D), jnp.bfloat16),
            pltpu.VMEM((ROWS, D), jnp.float32),
            pltpu.VMEM((ROWS, D), jnp.bfloat16),
            pltpu.VMEM((ROWS, 1), jnp.float32),
        ),
        in_specs=[pl.BlockSpec(memory_space=pl.ANY)] * 4
        + [pl.BlockSpec(memory_space=pltpu.SMEM)] * 2,
        out_specs=(fast,) * 4,
        scratch_shapes=[
            pltpu.VMEM((SPARE + ROWS, D), jnp.bfloat16),
            pltpu.VMEM((ROWS, D), jnp.bfloat16),
            pltpu.VMEM((ROWS, D), jnp.int32),
            pltpu.VMEM((labels.shape[0] // 128, 128), jnp.int32),
            pltpu.VMEM((ROWS, 128), jnp.int32),
            pltpu.VMEM((2, PAIRS, PAIR), jnp.int32),
            pltpu.VMEM((ROWS, 1), jnp.float32),
            pltpu.VMEM((ROWS, D), jnp.float32),
            pltpu.VMEM((2, ROWS, SET), jnp.bfloat16),
            dma((3, pieces)),
            dma,
            dma((2,)),
            dma((2,)),
            dma,
            dma((2 * UNIT,)),
            dma,
            dma((2 * HALVES,)),
            dma,
            dma((HALVES,)),
        ],
        compiler_params=pltpu.CompilerParams(
            collective_id=0, has_side_effects=True, vmem_limit_bytes=48 * 1024 * 1024
        ),
    )(
        *(
            pltpu.with_memory_space_constraint(array, pltpu.HBM)
            for array in (image_embed, text_embed, text_bits, labels.reshape(-1, 128))
        ),
        scale.reshape(1), bias.reshape(1),
    )
    block = jax.ShapeDtypeStruct((ROWS, D), jnp.bfloat16)
    return pl.pallas_call(
        finish_kernel,
        out_shape=(block, block),
        in_specs=[fast] * 4,
        out_specs=(pl.BlockSpec(memory_space=pl.ANY),) * 2,
        scratch_shapes=[pltpu.VMEM((ROWS, D), jnp.bfloat16), dma((pieces,)), dma],
        compiler_params=pltpu.CompilerParams(vmem_limit_bytes=16 * 1024 * 1024),
    )(*parts)


def solution(mesh):
    rows = P(("blk", "group"), None)
    return jax.shard_map(
        functools.partial(shards, mesh.shape["blk"], mesh.shape["group"]),
        mesh=mesh,
        in_specs=(rows, rows, rows, P(), P(), P()),
        out_specs=(rows, rows),
        check_vma=False,
    )
```

```python
import functools

import jax
import jax.numpy as jnp
from jax import lax
from jax.experimental import pallas as pl
from jax.experimental.pallas import tpu as pltpu
from jax.sharding import PartitionSpec as P

EPS = 1e-06
LOG2E = 1.4426950408889634
MESH = pl.DeviceIdType.MESH

ROWS = 640
D = 1152
HALF = 64
PAIR = 2 * HALF
SUB = 32
UNIT = ROWS // SUB
WIDE = 256
PREP = 128
LAST = 128
STEP = 32
SET = 4 * ROWS
SPARE = 2 * SET
LAB = ROWS // 128
HALVES = ROWS // HALF
PAIRS = SET // PAIR
CHUNK = 2 * PAIR


def kernel(
    n_blk,
    n_group,
    image_ref,
    text_ref,
    bits_ref,
    labels_ref,
    scale_ref,
    bias_ref,
    grad_text,
    sums_image,
    raw_image,
    inverse_image,
    along_image,
    last_coef,
    last_rows,
    held,
    raw_text,
    bits,
    labels,
    column,
    table,
    inverse_text,
    sums_text,
    along,
    coefs,
    load_sem,
    label_sem,
    lead_sem,
    near_send,
    near_recv,
    first_send,
    first_recv,
    far_send,
    far_recv,
    side_send,
    side_recv,
):
    b = lax.axis_index("blk")
    g = lax.axis_index("group")
    core = b % 2
    low = g % 2
    twin = b + 1 - 2 * core
    beyond = (b + 2 * core - 1 + n_blk) % n_blk
    mate = g + 1 - 2 * low
    side_to = (g + 2 - 4 * low + n_group) % n_group
    side_from = (g - 2 + 4 * low + n_group) % n_group
    near_dev, first_dev = (twin, g), (b, mate)
    far_dev, side_dev, source_dev = (beyond, mate), (b, side_to), (b, side_from)

    def lead_copy(start, stop, sem):
        rows = pl.ds(start, stop - start)
        return pltpu.make_async_copy(image_ref.at[rows], raw_image.at[rows], sem)

    leads = (
        lead_copy(0, STEP, lead_sem.at[0]),
        lead_copy(STEP, PREP, lead_sem.at[1]),
    )
    leads[0].start()
    leads[1].start()

    barrier = pltpu.get_barrier_semaphore()
    for device in (near_dev, first_dev, far_dev, source_dev):
        pl.semaphore_signal(barrier, inc=1, device_id=device, device_id_type=MESH)

    def load(array, to, piece, sems):
        rows = pl.ds(piece * PREP, PREP)
        return pltpu.make_async_copy(array.at[rows], to.at[rows], sems.at[piece])

    pieces = ROWS // PREP
    loads = ((image_ref, raw_image), (text_ref, raw_text), (bits_ref, bits))

    def start_loads():
        for which, (array, to) in enumerate(loads):
            for piece in range(1 if which == 0 else 0, pieces):
                load(array, to, piece, load_sem.at[which]).start()
        label_copy.start()

    label_copy = pltpu.make_async_copy(labels_ref, labels, label_sem)
    def remote(src, dst, send, recv, device):
        return pltpu.make_async_remote_copy(
            src_ref=held.at[src],
            dst_ref=held.at[dst],
            send_sem=send,
            recv_sem=recv,
            device_id=device,
            device_id_type=MESH,
        )

    def span(start, size):
        return pl.ds(pl.multiple_of(start, 16), size)

    def landing(h):
        texts = h // UNIT
        at = h - texts * UNIT
        half = at // (HALF // SUB)
        inside = (at - half * (HALF // SUB)) * SUB
        return texts, half, (1 - texts) * SET + 2 * ROWS + half * PAIR + inside

    def first_row(h, to_low):
        texts, _, row = landing(h)
        at = h - texts * UNIT
        used = texts * to_low + (1 - texts) * (1 - to_low)
        return used * (row + HALF) + (1 - used) * (SPARE + at * SUB)

    def first(h):
        texts = h // UNIT
        at = h - texts * UNIT
        return remote(
            span((1 - texts) * SET + at * SUB, SUB),
            span(first_row(h, 1 - low), SUB),
            first_send,
            first_recv.at[h],
            first_dev,
        )

    def far(h):
        texts, half, row = landing(h)
        return remote(
            span(first_row(h, low), SUB),
            span(row, SUB),
            far_send,
            far_recv.at[texts * HALVES + half],
            far_dev,
        )

    def side(h):
        texts, half, row = landing(h)
        return remote(
            span(first_row(h, low), SUB),
            span(row + HALF, SUB),
            side_send,
            side_recv.at[half],
            side_dev,
        )

    def near(texts):
        start = (1 - texts) * SET
        return remote(
            span(start, ROWS),
            span(start + ROWS, ROWS),
            near_send.at[texts],
            near_recv.at[texts],
            near_dev,
        )

    def unit_rows(fulls, steps, inverse, base):
        invs = [
            lax.rsqrt(jnp.sum(jnp.square(full()), axis=-1, keepdims=True) + EPS) for full in fulls
        ]
        for full, inv, row in zip(fulls, invs, steps):
            inverse[pl.ds(row, STEP), :] = inv
            held[pl.ds(base + row, STEP), :] = (full() * inv).astype(jnp.bfloat16)

    def steps_of(row, size):
        return [pl.multiple_of(row + at, STEP) for at in range(0, size, STEP)]

    def loader(array, row):
        return lambda: array[pl.ds(row, STEP), :].astype(jnp.float32)

    def image_rows(row, size):
        steps = steps_of(row, size)
        unit_rows([loader(raw_image, at) for at in steps], steps, inverse_image, SET)

    def text_rows(row, size):
        steps = steps_of(row, size)
        for at in steps:
            rows = pl.ds(at, STEP)
            noise = (bits[rows, :].astype(jnp.float32) + 0.5) * (1.0 / 4096.0)
            full = jnp.floor(raw_text[rows, :].astype(jnp.float32) * 128.0 + noise) * (1.0 / 128.0)
            raw_text[rows, :] = full.astype(jnp.bfloat16)
        unit_rows([loader(raw_text, at) for at in steps], steps, inverse_text, 0)

    per = PREP // SUB

    def send(h, _):
        first(h).start()
        return 0

    leads[0].wait()
    image_rows(0, STEP)
    pl.semaphore_wait(barrier, 4)
    lax.fori_loop(0, STEP // SUB, send, 0)
    start_loads()
    leads[1].wait()
    for row in range(STEP, PREP, STEP):
        image_rows(row, STEP)
        lax.fori_loop(row // SUB, (row + STEP) // SUB, send, 0)

    def image_step(piece, _):
        load(image_ref, raw_image, piece, load_sem.at[0]).wait()
        image_rows(piece * PREP, PREP)
        lax.fori_loop(piece * per, (piece + 1) * per, send, 0)
        return 0

    lax.fori_loop(1, pieces, image_step, 0)
    near(0).start()

    def pump(h):
        first(h).wait_recv()

        @pl.when(h // UNIT == 1 - low)
        def _():
            side(h).start()

        far(h).start()

    def pumps(start, stop):
        def one(h, _):
            pump(h)
            return 0

        lax.fori_loop(start, stop, one, 0)

    pumps(0, 1)

    def text_step(piece, _):
        load(text_ref, raw_text, piece, load_sem.at[1]).wait()
        load(bits_ref, bits, piece, load_sem.at[2]).wait()
        text_rows(piece * PREP, PREP)
        lax.fori_loop(UNIT + piece * per, UNIT + (piece + 1) * per, send, 0)

        @pl.when(piece % 2 == 0)
        def _():
            pump(1 + piece // 2)

        return 0

    lax.fori_loop(0, pieces, text_step, 0)
    near(1).start()

    label_copy.wait()
    number = b * n_group + g
    for part in range(LAB):
        row = jnp.broadcast_to(labels[pl.ds(number * LAB + part, 1), :], (128, 128))
        column[pl.ds(part * 128, 128), :] = row.T

    below = (g - 1 + n_group) % n_group
    above = (g + 1) % n_group
    first_half = lax.broadcasted_iota(jnp.int32, (1, PAIR), 1) < HALF

    def label_row(at_blk, at_group, part):
        return labels[pl.ds((at_blk * n_group + at_group) * LAB + part, 1), :]

    for which, other in ((0, below), (1, above)):
        for part in range(LAB):
            table[which, pl.ds(part, 1), :] = label_row(b, g, part)
            table[which, pl.ds(LAB + part, 1), :] = label_row(twin, g, part)
            far_labels = label_row(beyond, g, part)
            group_labels = label_row(b, other, part)
            table[which, pl.ds(2 * LAB + 2 * part, 1), :] = jnp.where(
                first_half, far_labels, pltpu.roll(group_labels, HALF, 1)
            )
            table[which, pl.ds(2 * LAB + 2 * part + 1, 1), :] = jnp.where(
                first_half, pltpu.roll(far_labels, HALF, 1), group_labels
            )

    scale = scale_ref[0]
    slope = scale * LOG2E
    shift = bias_ref[0] * LOG2E

    def meet(which, at, size, last=False):
        them_rows = span(which * SET + at * PAIR, size)
        own_rows = span((1 - which) * SET, ROWS)
        dots = lax.dot_general(
            held[own_rows, :],
            held[them_rows, :],
            (((1,), (1,)), ((), ())),
            preferred_element_type=jnp.float32,
        )
        power = dots * slope + shift
        mine = column[...]
        same = [mine == table[which, pl.ds(at + i, 1), :] for i in range(size // PAIR)]
        same = same[0] if size == PAIR else jnp.concatenate(same, axis=1)
        coef = jnp.where(same, -scale, scale) / (1.0 + jnp.exp2(jnp.where(same, power, -power)))
        coef = coef.astype(jnp.bfloat16)
        share = coef.astype(jnp.float32) * dots
        share = share[:, :PAIR] + share[:, PAIR:] if size == CHUNK else share
        if last:
            last_coef[...] = coef
            along_image[...] = along[which] + share
        else:
            columns = pl.ds(pl.multiple_of(at * PAIR, PAIR), size)
            coefs[which, :, columns] = coef
            along[which] += share

    def add_up(which, start, stop, column_at, width, fresh):
        rows = (stop - start) * PAIR
        columns = pl.ds(pl.multiple_of(column_at, 128), width)
        sums = lax.dot_general(
            coefs[which, :, pl.ds(start * PAIR, rows)],
            held[pl.ds(which * SET + start * PAIR, rows), columns],
            (((1,), (0,)), ((), ())),
            preferred_element_type=jnp.float32,
        )
        total = (sums_image, sums_text)[which]
        if not fresh:
            sums = sums + total[:, columns]
        total[:, columns] = sums

    full_columns = D // WIDE
    rest = D - full_columns * WIDE

    def whole(start, size, send, recv):
        return remote(span(start, size), span(start, size), send, recv, first_dev)

    def landed(texts, k):
        base = (1 - texts) * SET + 2 * ROWS + k * PAIR
        whole(base, HALF, far_send, far_recv.at[texts * HALVES + k]).wait_recv()

        @pl.when(low == 1 - texts)
        def _():
            whole(base + HALF, HALF, side_send, side_recv.at[k]).wait_recv()

    def meet_far(texts, k):
        landed(texts, 2 * k)
        landed(texts, 2 * k + 1)
        meet(1 - texts, 2 * LAB + 2 * k, CHUNK)

    along[...] = jnp.zeros_like(along)

    def early(p, _):
        pump(4 + p)

        @pl.when(p == 4)
        def _():
            near(0).wait_recv()
            near(1).wait_recv()

        meet(1 - p % 2, 2 * (p // 2), CHUNK)
        return 0

    lax.fori_loop(0, 2 * LAB, early, 0)

    def far_images(k, _):
        pump(14 + k)
        meet_far(0, k)
        return 0

    lax.fori_loop(0, 3, far_images, 0)
    pumps(17, 19)

    def far_images_end(k, _):
        pumps(19 + 2 * (k - 3), 21 + 2 * (k - 3))
        meet_far(0, k)
        return 0

    lax.fori_loop(3, LAB, far_images_end, 0)

    def text_sums(n, _):
        pump(23 + n)
        add_up(1, 0, PAIRS, n * WIDE, WIDE, True)
        return 0

    lax.fori_loop(0, full_columns, text_sums, 0)
    pumps(27, 28)
    add_up(1, 0, PAIRS, full_columns * WIDE, rest, True)

    def text_out(piece, _):
        @pl.when(piece % 2 == 0)
        def _():
            pump(28 + piece // 2)

        for at in range(0, PREP, STEP):
            finish_rows(raw_text, inverse_text, along.at[1], sums_text, grad_text, piece * PREP + at, STEP)
        return 0

    lax.fori_loop(0, pieces, text_out, 0)

    def far_texts(k, _):
        pump(31 + k)
        meet_far(1, k)
        return 0

    lax.fori_loop(0, 3, far_texts, 0)

    def image_sums(n, _):
        pump(34 + n)
        add_up(0, 0, PAIRS - 4, n * WIDE, WIDE, True)
        return 0

    lax.fori_loop(0, full_columns, image_sums, 0)
    pumps(38, 40)
    add_up(0, 0, PAIRS - 4, full_columns * WIDE, rest, True)

    meet_far(1, LAB - 2)
    landed(1, HALVES - 2)
    meet(0, PAIRS - 2, PAIR)
    add_up(0, PAIRS - 4, PAIRS - 1, 0, D, False)
    landed(1, HALVES - 1)
    last_rows[...] = held[SET - PAIR : SET, :]
    meet(0, PAIRS - 1, PAIR, last=True)

    near(0).wait_send()
    near(1).wait_send()
    whole(0, 2 * ROWS, first_send, first_recv.at[0]).wait_send()
    whole(0, 2 * ROWS, far_send, first_recv.at[0]).wait_send()
    whole(0, ROWS, side_send, first_recv.at[0]).wait_send()


def finish_rows(raw, inverse, along, sums, out, row, size, more=None):
    rows = pl.ds(pl.multiple_of(row, STEP), size)
    inv = inverse[rows, :]
    share = inv * jnp.sum(along[rows, :], axis=-1, keepdims=True)
    total = sums[rows, :]
    if more is not None:
        total = total + more(rows)
    full = raw[rows, :].astype(jnp.float32)
    out[rows, :] = ((total - full * share) * inv).astype(jnp.bfloat16)


def finish_kernel(
    text, sums, raw, inverse, along, coef, others, image_out, text_out, image, store_sem, text_sem
):
    whole = pltpu.make_async_copy(text, text_out, text_sem)
    whole.start()

    def store(piece):
        rows = pl.ds(piece * LAST, LAST)
        return pltpu.make_async_copy(image.at[rows], image_out.at[rows], store_sem.at[piece])

    def more(rows):
        return jnp.dot(coef[rows, :], others[...], preferred_element_type=jnp.float32)

    pieces = ROWS // LAST
    for piece in range(pieces):
        finish_rows(raw, inverse, along, sums, image, piece * LAST, LAST, more)
        store(piece).start()
    whole.wait()
    for piece in range(pieces):
        store(piece).wait()


def shards(n_blk, n_group, image_embed, text_embed, text_bits, labels, scale, bias):
    dma = pltpu.SemaphoreType.DMA
    pieces = ROWS // PREP
    fast = pl.BlockSpec(memory_space=pltpu.VMEM)
    parts = pl.pallas_call(
        functools.partial(kernel, n_blk, n_group),
        out_shape=(
            pltpu.VMEM((ROWS, D), jnp.bfloat16),
            pltpu.VMEM((ROWS, D), jnp.float32),
            pltpu.VMEM((ROWS, D), jnp.bfloat16),
            pltpu.VMEM((ROWS, 1), jnp.float32),
            pltpu.VMEM((ROWS, PAIR), jnp.float32),
            pltpu.VMEM((ROWS, PAIR), jnp.bfloat16),
            pltpu.VMEM((PAIR, D), jnp.bfloat16),
        ),
        in_specs=[pl.BlockSpec(memory_space=pl.ANY)] * 4
        + [pl.BlockSpec(memory_space=pltpu.SMEM)] * 2,
        out_specs=(fast,) * 7,
        scratch_shapes=[
            pltpu.VMEM((SPARE + ROWS, D), jnp.bfloat16),
            pltpu.VMEM((ROWS, D), jnp.bfloat16),
            pltpu.VMEM((ROWS, D), jnp.int32),
            pltpu.VMEM((labels.shape[0] // 128, 128), jnp.int32),
            pltpu.VMEM((ROWS, 128), jnp.int32),
            pltpu.VMEM((2, PAIRS, PAIR), jnp.int32),
            pltpu.VMEM((ROWS, 1), jnp.float32),
            pltpu.VMEM((ROWS, D), jnp.float32),
            pltpu.VMEM((2, ROWS, PAIR), jnp.float32),
            pltpu.VMEM((2, ROWS, SET), jnp.bfloat16),
            dma((3, pieces)),
            dma,
            dma((2,)),
            dma((2,)),
            dma((2,)),
            dma,
            dma((2 * UNIT,)),
            dma,
            dma((2 * HALVES,)),
            dma,
            dma((HALVES,)),
        ],
        compiler_params=pltpu.CompilerParams(
            collective_id=0, has_side_effects=True, vmem_limit_bytes=48 * 1024 * 1024
        ),
    )(
        *(
            pltpu.with_memory_space_constraint(array, pltpu.HBM)
            for array in (image_embed, text_embed, text_bits, labels.reshape(-1, 128))
        ),
        scale.reshape(1), bias.reshape(1),
    )
    block = jax.ShapeDtypeStruct((ROWS, D), jnp.bfloat16)
    return pl.pallas_call(
        finish_kernel,
        out_shape=(block, block),
        in_specs=[fast] * 7,
        out_specs=(pl.BlockSpec(memory_space=pl.ANY),) * 2,
        scratch_shapes=[pltpu.VMEM((ROWS, D), jnp.bfloat16), dma((ROWS // LAST,)), dma],
        compiler_params=pltpu.CompilerParams(vmem_limit_bytes=16 * 1024 * 1024),
    )(*parts)


def solution(mesh):
    rows = P(("blk", "group"), None)
    return jax.shard_map(
        functools.partial(shards, mesh.shape["blk"], mesh.shape["group"]),
        mesh=mesh,
        in_specs=(rows, rows, rows, P(), P(), P()),
        out_specs=(rows, rows),
        check_vma=False,
    )
```

```python
import functools

import jax
import jax.numpy as jnp
from jax import lax
from jax.experimental import pallas as pl
from jax.experimental.pallas import tpu as pltpu
from jax.sharding import PartitionSpec as P

EPS = 1e-06
LOG2E = 1.4426950408889634
MESH = pl.DeviceIdType.MESH

ROWS = 640
D = 1152
HALF = 64
PAIR = 2 * HALF
SUB = 32
UNIT = ROWS // SUB
LEAD = 2
WIDE = 256
PREP = 128
STEP = 32
SET = 4 * ROWS
SPARE = 2 * SET
LAB = ROWS // 128
HALVES = ROWS // HALF
PAIRS = SET // PAIR
CHUNK = 2 * PAIR


def kernel(
    n_blk,
    n_group,
    image_ref,
    text_ref,
    bits_ref,
    labels_ref,
    scale_ref,
    bias_ref,
    grad_text,
    sums_image,
    raw_image,
    inverse_image,
    held,
    raw_text,
    bits,
    labels,
    column,
    table,
    inverse_text,
    sums_text,
    coefs,
    load_sem,
    label_sem,
    near_send,
    near_recv,
    go_sem,
    first_send,
    first_recv,
    far_send,
    far_recv,
    side_send,
    side_recv,
):
    b = lax.axis_index("blk")
    g = lax.axis_index("group")
    core = b % 2
    low = g % 2
    twin = b + 1 - 2 * core
    beyond = (b + 2 * core - 1 + n_blk) % n_blk
    mate = g + 1 - 2 * low
    side_to = (g + 2 - 4 * low + n_group) % n_group
    side_from = (g - 2 + 4 * low + n_group) % n_group
    near_dev, first_dev = (twin, g), (b, mate)
    far_dev, side_dev, source_dev = (beyond, mate), (b, side_to), (b, side_from)

    barrier = pltpu.get_barrier_semaphore()
    for device in (near_dev, first_dev, far_dev, source_dev):
        pl.semaphore_signal(barrier, inc=1, device_id=device, device_id_type=MESH)

    def load(array, to, piece, sems):
        rows = pl.ds(piece * PREP, PREP)
        return pltpu.make_async_copy(array.at[rows], to.at[rows], sems.at[piece])

    pieces = ROWS // PREP
    loads = ((image_ref, raw_image), (text_ref, raw_text), (bits_ref, bits))
    for which, (array, to) in enumerate(loads):
        for piece in range(pieces):
            load(array, to, piece, load_sem.at[which]).start()
    label_copy = pltpu.make_async_copy(labels_ref, labels, label_sem)
    label_copy.start()

    def remote(src, dst, send, recv, device):
        return pltpu.make_async_remote_copy(
            src_ref=held.at[src],
            dst_ref=held.at[dst],
            send_sem=send,
            recv_sem=recv,
            device_id=device,
            device_id_type=MESH,
        )

    def span(start, size):
        return pl.ds(pl.multiple_of(start, 16), size)

    def landing(h):
        texts = h // UNIT
        at = h - texts * UNIT
        half = at // (HALF // SUB)
        inside = (at - half * (HALF // SUB)) * SUB
        return texts, half, (1 - texts) * SET + 2 * ROWS + half * PAIR + inside

    def first_row(h, to_low):
        texts, _, row = landing(h)
        at = h - texts * UNIT
        used = texts * to_low + (1 - texts) * (1 - to_low)
        return used * (row + HALF) + (1 - used) * (SPARE + at * SUB)

    def first(h):
        texts = h // UNIT
        at = h - texts * UNIT
        return remote(
            span((1 - texts) * SET + at * SUB, SUB),
            span(first_row(h, 1 - low), SUB),
            first_send.at[(h + 2 * UNIT - LEAD) // (2 * UNIT)],
            first_recv.at[h],
            first_dev,
        )

    def far(h):
        texts, half, row = landing(h)
        return remote(
            span(first_row(h, low), SUB),
            span(row, SUB),
            far_send,
            far_recv.at[texts * HALVES + half],
            far_dev,
        )

    def side(h):
        texts, half, row = landing(h)
        return remote(
            span(first_row(h, low), SUB),
            span(row + HALF, SUB),
            side_send,
            side_recv.at[half],
            side_dev,
        )

    def whole(start, size, send, recv):
        return remote(span(start, size), span(start, size), send, recv, first_dev)

    def near(texts):
        start = (1 - texts) * SET
        return remote(
            span(start, ROWS),
            span(start + ROWS, ROWS),
            near_send.at[texts],
            near_recv.at[texts],
            near_dev,
        )

    def unit_rows(fulls, steps, inverse, base):
        invs = [
            lax.rsqrt(jnp.sum(jnp.square(full()), axis=-1, keepdims=True) + EPS) for full in fulls
        ]
        for full, inv, row in zip(fulls, invs, steps):
            inverse[pl.ds(row, STEP), :] = inv
            held[pl.ds(base + row, STEP), :] = (full() * inv).astype(jnp.bfloat16)

    def steps_of(row, size):
        return [pl.multiple_of(row + at, STEP) for at in range(0, size, STEP)]

    def loader(array, row):
        return lambda: array[pl.ds(row, STEP), :].astype(jnp.float32)

    def image_rows(row, size):
        steps = steps_of(row, size)
        unit_rows([loader(raw_image, at) for at in steps], steps, inverse_image, SET)

    def text_rows(row, size):
        steps = steps_of(row, size)
        for at in steps:
            rows = pl.ds(at, STEP)
            noise = (bits[rows, :].astype(jnp.float32) + 0.5) * (1.0 / 4096.0)
            full = jnp.floor(raw_text[rows, :].astype(jnp.float32) * 128.0 + noise) * (1.0 / 128.0)
            raw_text[rows, :] = full.astype(jnp.bfloat16)
        unit_rows([loader(raw_text, at) for at in steps], steps, inverse_text, 0)

    per = PREP // SUB

    def send(h, _):
        first(h).start()
        return 0

    load(image_ref, raw_image, 0, load_sem.at[0]).wait()
    image_rows(0, STEP)
    pl.semaphore_wait(barrier, 4)

    leads = b == 2
    follows = b == 3

    @pl.when(follows)
    def _():
        pl.semaphore_wait(go_sem, 1)

    lax.fori_loop(0, STEP // SUB, send, 0)
    for row in range(STEP, PREP, STEP):
        image_rows(row, STEP)
        lax.fori_loop(row // SUB, (row + STEP) // SUB, send, 0)

    @pl.when(leads)
    def _():
        whole(0, LEAD * SUB, first_send.at[0], first_recv.at[0]).wait_send()
        pl.semaphore_signal(go_sem, inc=1, device_id=near_dev, device_id_type=MESH)

    def image_step(piece, _):
        load(image_ref, raw_image, piece, load_sem.at[0]).wait()
        image_rows(piece * PREP, PREP)
        lax.fori_loop(piece * per, (piece + 1) * per, send, 0)
        return 0

    lax.fori_loop(1, pieces, image_step, 0)

    @pl.when(jnp.logical_not(leads))
    def _():
        whole(0, LEAD * SUB, first_send.at[0], first_recv.at[0]).wait_send()

    near(0).start()

    def pump(h):
        first(h).wait_recv()
        far(h).start()

        @pl.when(h // UNIT == 1 - low)
        def _():
            side(h).start()

    def pumps(start, stop):
        def one(h, _):
            pump(h)
            return 0

        lax.fori_loop(start, stop, one, 0)

    pumps(0, 1)

    def text_step(piece, _):
        load(text_ref, raw_text, piece, load_sem.at[1]).wait()
        load(bits_ref, bits, piece, load_sem.at[2]).wait()
        text_rows(piece * PREP, PREP)
        lax.fori_loop(UNIT + piece * per, UNIT + (piece + 1) * per, send, 0)

        @pl.when(piece % 2 == 0)
        def _():
            pump(1 + piece // 2)

        return 0

    lax.fori_loop(0, pieces, text_step, 0)
    near(1).start()

    label_copy.wait()
    number = b * n_group + g
    for part in range(LAB):
        row = jnp.broadcast_to(labels[pl.ds(number * LAB + part, 1), :], (128, 128))
        column[pl.ds(part * 128, 128), :] = row.T

    below = (g - 1 + n_group) % n_group
    above = (g + 1) % n_group
    first_half = lax.broadcasted_iota(jnp.int32, (1, PAIR), 1) < HALF

    def label_row(at_blk, at_group, part):
        return labels[pl.ds((at_blk * n_group + at_group) * LAB + part, 1), :]

    for which, other in ((0, below), (1, above)):
        for part in range(LAB):
            table[which, pl.ds(part, 1), :] = label_row(b, g, part)
            table[which, pl.ds(LAB + part, 1), :] = label_row(twin, g, part)
            far_labels = label_row(beyond, g, part)
            group_labels = label_row(b, other, part)
            table[which, pl.ds(2 * LAB + 2 * part, 1), :] = jnp.where(
                first_half, far_labels, pltpu.roll(group_labels, HALF, 1)
            )
            table[which, pl.ds(2 * LAB + 2 * part + 1, 1), :] = jnp.where(
                first_half, pltpu.roll(far_labels, HALF, 1), group_labels
            )

    scale = scale_ref[0]
    slope = scale * LOG2E
    shift = bias_ref[0] * LOG2E

    def meet(which, at, size):
        them_rows = span(which * SET + at * PAIR, size)
        own_rows = span((1 - which) * SET, ROWS)
        dots = lax.dot_general(
            held[own_rows, :],
            held[them_rows, :],
            (((1,), (1,)), ((), ())),
            preferred_element_type=jnp.float32,
        )
        power = dots * slope + shift
        mine = column[...]
        same = [mine == table[which, pl.ds(at + i, 1), :] for i in range(size // PAIR)]
        same = same[0] if size == PAIR else jnp.concatenate(same, axis=1)
        coef = jnp.where(same, -scale, scale) / (1.0 + jnp.exp2(jnp.where(same, power, -power)))
        columns = pl.ds(pl.multiple_of(at * PAIR, PAIR), size)
        coefs[which, :, columns] = coef.astype(jnp.bfloat16)

    def add_up(which, start, stop, column_at, width, fresh):
        rows = (stop - start) * PAIR
        columns = pl.ds(pl.multiple_of(column_at, 128), width)
        sums = lax.dot_general(
            coefs[which, :, pl.ds(start * PAIR, rows)],
            held[pl.ds(which * SET + start * PAIR, rows), columns],
            (((1,), (0,)), ((), ())),
            preferred_element_type=jnp.float32,
        )
        total = (sums_image, sums_text)[which]
        if not fresh:
            sums = sums + total[:, columns]
        total[:, columns] = sums

    full_columns = D // WIDE
    rest = D - full_columns * WIDE

    def landed(texts, k):
        base = (1 - texts) * SET + 2 * ROWS + k * PAIR
        whole(base, HALF, far_send, far_recv.at[texts * HALVES + k]).wait_recv()

        @pl.when(low == 1 - texts)
        def _():
            whole(base + HALF, HALF, side_send, side_recv.at[k]).wait_recv()

    def meet_far(texts, k):
        landed(texts, 2 * k)
        landed(texts, 2 * k + 1)
        meet(1 - texts, 2 * LAB + 2 * k, CHUNK)

    def early(p, _):
        pump(4 + p)

        @pl.when(p == 4)
        def _():
            near(0).wait_recv()
            near(1).wait_recv()

        meet(1 - p % 2, 2 * (p // 2), CHUNK)
        return 0

    lax.fori_loop(0, 2 * LAB, early, 0)

    def far_images(k, _):
        pump(14 + k)
        meet_far(0, k)
        return 0

    lax.fori_loop(0, 3, far_images, 0)
    pumps(17, 19)

    def far_images_end(k, _):
        pumps(19 + 2 * (k - 3), 21 + 2 * (k - 3))
        meet_far(0, k)
        return 0

    lax.fori_loop(3, LAB, far_images_end, 0)

    def text_sums(n, _):
        pump(23 + n)
        add_up(1, 0, PAIRS, n * WIDE, WIDE, True)
        return 0

    lax.fori_loop(0, full_columns, text_sums, 0)
    pumps(27, 28)
    add_up(1, 0, PAIRS, full_columns * WIDE, rest, True)

    def text_out(piece, _):
        @pl.when(piece % 2 == 0)
        def _():
            pump(28 + piece // 2)

        finish_rows(raw_text, inverse_text, sums_text, grad_text, piece * PREP)
        return 0

    lax.fori_loop(0, pieces, text_out, 0)

    def far_texts(k, _):
        pump(31 + k)
        meet_far(1, k)
        return 0

    lax.fori_loop(0, 3, far_texts, 0)

    def image_sums(n, _):
        pump(34 + n)
        add_up(0, 0, PAIRS - 4, n * WIDE, WIDE, True)
        return 0

    lax.fori_loop(0, full_columns, image_sums, 0)
    pumps(38, 40)
    add_up(0, 0, PAIRS - 4, full_columns * WIDE, rest, True)

    meet_far(1, LAB - 2)
    landed(1, HALVES - 2)
    meet(0, PAIRS - 2, PAIR)
    add_up(0, PAIRS - 4, PAIRS - 1, 0, D, False)
    landed(1, HALVES - 1)
    meet(0, PAIRS - 1, PAIR)
    add_up(0, PAIRS - 1, PAIRS, 0, D, False)

    near(0).wait_send()
    near(1).wait_send()
    whole(0, 2 * ROWS - LEAD * SUB, first_send.at[1], first_recv.at[0]).wait_send()
    whole(0, 2 * ROWS, far_send, first_recv.at[0]).wait_send()
    whole(0, ROWS, side_send, first_recv.at[0]).wait_send()


def finish_rows(raw, inverse, sums, out, row):
    steps = [pl.ds(pl.multiple_of(row + at, STEP), STEP) for at in range(0, PREP, STEP)]
    along = []
    for rows in steps:
        inv = inverse[rows, :]
        dot = jnp.sum(raw[rows, :].astype(jnp.float32) * sums[rows, :], axis=-1, keepdims=True)
        along.append((inv, inv * inv * dot))
    for rows, (inv, share) in zip(steps, along):
        full = raw[rows, :].astype(jnp.float32)
        out[rows, :] = ((sums[rows, :] - full * share) * inv).astype(jnp.bfloat16)


def finish_kernel(text, sums, raw, inverse, image_out, text_out, image, store_sem, text_sem):
    whole = pltpu.make_async_copy(text, text_out, text_sem)
    whole.start()

    def store(piece):
        rows = pl.ds(piece * PREP, PREP)
        return pltpu.make_async_copy(image.at[rows], image_out.at[rows], store_sem.at[piece])

    pieces = ROWS // PREP
    for piece in range(pieces):
        finish_rows(raw, inverse, sums, image, piece * PREP)
        store(piece).start()
    whole.wait()
    for piece in range(pieces):
        store(piece).wait()


def shards(n_blk, n_group, image_embed, text_embed, text_bits, labels, scale, bias):
    dma = pltpu.SemaphoreType.DMA
    pieces = ROWS // PREP
    fast = pl.BlockSpec(memory_space=pltpu.VMEM)
    parts = pl.pallas_call(
        functools.partial(kernel, n_blk, n_group),
        out_shape=(
            pltpu.VMEM((ROWS, D), jnp.bfloat16),
            pltpu.VMEM((ROWS, D), jnp.float32),
            pltpu.VMEM((ROWS, D), jnp.bfloat16),
            pltpu.VMEM((ROWS, 1), jnp.float32),
        ),
        in_specs=[pl.BlockSpec(memory_space=pl.ANY)] * 4
        + [pl.BlockSpec(memory_space=pltpu.SMEM)] * 2,
        out_specs=(fast,) * 4,
        scratch_shapes=[
            pltpu.VMEM((SPARE + ROWS, D), jnp.bfloat16),
            pltpu.VMEM((ROWS, D), jnp.bfloat16),
            pltpu.VMEM((ROWS, D), jnp.int32),
            pltpu.VMEM((labels.shape[0] // 128, 128), jnp.int32),
            pltpu.VMEM((ROWS, 128), jnp.int32),
            pltpu.VMEM((2, PAIRS, PAIR), jnp.int32),
            pltpu.VMEM((ROWS, 1), jnp.float32),
            pltpu.VMEM((ROWS, D), jnp.float32),
            pltpu.VMEM((2, ROWS, SET), jnp.bfloat16),
            dma((3, pieces)),
            dma,
            dma((2,)),
            dma((2,)),
            pltpu.SemaphoreType.REGULAR,
            dma((2,)),
            dma((2 * UNIT,)),
            dma,
            dma((2 * HALVES,)),
            dma,
            dma((HALVES,)),
        ],
        compiler_params=pltpu.CompilerParams(
            collective_id=0, has_side_effects=True, vmem_limit_bytes=48 * 1024 * 1024
        ),
    )(
        *(
            pltpu.with_memory_space_constraint(array, pltpu.HBM)
            for array in (image_embed, text_embed, text_bits, labels.reshape(-1, 128))
        ),
        scale.reshape(1), bias.reshape(1),
    )
    block = jax.ShapeDtypeStruct((ROWS, D), jnp.bfloat16)
    return pl.pallas_call(
        finish_kernel,
        out_shape=(block, block),
        in_specs=[fast] * 4,
        out_specs=(pl.BlockSpec(memory_space=pl.ANY),) * 2,
        scratch_shapes=[pltpu.VMEM((ROWS, D), jnp.bfloat16), dma((pieces,)), dma],
        compiler_params=pltpu.CompilerParams(vmem_limit_bytes=16 * 1024 * 1024),
    )(*parts)


def solution(mesh):
    rows = P(("blk", "group"), None)
    return jax.shard_map(
        functools.partial(shards, mesh.shape["blk"], mesh.shape["group"]),
        mesh=mesh,
        in_specs=(rows, rows, rows, P(), P(), P()),
        out_specs=(rows, rows),
        check_vma=False,
    )
```
